32 devices in a mesh: img: 8 (over y, x, core), view: 4 (over z).
Axes of the slice: x: 2, y: 2, z: 4, core: 2. Of those that a mesh axis runs over, the one named last changes fastest.
Arguments:
- images: float32 [2, 3072, 1024], P(None, ('img', 'view')), may hold values from -30 to 30, as said below
- views: float32 [2048, 1024], P('view'), may hold values from -5 to 5, as said below
Outputs:
- new_views: float32 [2048, 1024], P('view')
The draws below stay inside these ranges and needn't reach their ends.
Inputs may be any that keep to these rules, and one draw needn't show every extreme that they name: `images`: real valued Fourier values. `views`: real valued Fourier values.
All inputs are finite; a program needn't handle non-finite values.
Results may differ from the reference program's by a relative error of at most 0.0003.
Values sent between devices are 32-bit elements; how exact they have to be, the bound alone decides.
A program may use at most 64 MiB of HBM per device.

```python
import jax
import jax.numpy as jnp
from jax import lax

F = 1024
BATCH = 384
INNER = 2
ROUNDS = 1
VIEWS = 2048
IMAGES = 3072
N_IMG = 8


def common_views(key):
    base_views = jnp.clip(jax.random.normal(jax.random.fold_in(key, 1), (VIEWS, F), jnp.float32), -4.5, 4.5)
    return base_views


def draw_views(key, part):
    return common_views(jax.random.fold_in(key, 11))


def draw_images(key, part):
    pictures = jnp.clip(jax.random.normal(jax.random.fold_in(key, 21), (INNER * IMAGES, F), jnp.float32), -5.0, 5.0)
    return pictures.reshape(INNER, IMAGES, F)


def setup_inputs(seed: int = 0) -> dict:
    keys = jax.random.split(jax.random.key(seed), 3)
    return {
        "images": draw_images(jax.random.fold_in(keys[2], 71), 0),
        "views": draw_views(jax.random.fold_in(keys[2], 71), 0),
    }


def reference(images, views):
    beta = 1.6 / jnp.sqrt(jnp.float32(F))
    current = views
    for em_round in range(ROUNDS):
        half_norm = 0.5 * lax.optimization_barrier(jnp.sum(current * current, axis=1))

        def group_step(carry, group_id):
            res_acc, mass_acc = carry
            start = (group_id * BATCH).astype(jnp.int32)
            group_rows = lax.dynamic_slice_in_dim(images, start, BATCH, 1).reshape(INNER * BATCH, F)
            scores = beta * (jnp.dot(group_rows, current.T, precision=lax.Precision.HIGHEST) - half_norm)
            peak = lax.optimization_barrier(jnp.max(scores, axis=1, keepdims=True))
            expo = jnp.exp(scores - peak)
            post = expo / lax.optimization_barrier(jnp.sum(expo, axis=1, keepdims=True))
            numerator = jnp.dot(post.T, group_rows, precision=lax.Precision.HIGHEST)
            weight_mass = lax.optimization_barrier(jnp.sum(post, axis=0))
            residual_sum = numerator - weight_mass[:, None] * current
            return ((res_acc + residual_sum, mass_acc + weight_mass), None)
        start_carry = (jnp.zeros((VIEWS, F), jnp.float32), jnp.zeros((VIEWS,), jnp.float32))
        (res_total, mass_total), unused = lax.scan(group_step, start_carry, jnp.arange(N_IMG, dtype=jnp.int32))
        current = current + res_total / (mass_total[:, None] + 1.0)
    return current
```

```python
import functools
import math

import jax
import jax.numpy as jnp
from jax import lax
from jax.experimental import pallas as pl
from jax.experimental.pallas import tpu as pltpu
from jax.sharding import PartitionSpec as P

MESH = pl.DeviceIdType.MESH
F32 = jnp.float32
BF16 = jnp.bfloat16


def snake(c):
    row, col = c // 2, c % 2
    return 2 * row + col + (row % 2) * (1 - 2 * col)


def split(x):
    hi = x.astype(BF16)
    return hi, (x - hi.astype(F32)).astype(BF16)


def dot_nt(a, b):
    return lax.dot_general(a, b, (((1,), (1,)), ((), ())), preferred_element_type=F32)


def dot_nn(a, b):
    return lax.dot_general(a, b, (((1,), (0,)), ((), ())), preferred_element_type=F32)


class Ring:
    def __init__(self, chips, pos, core, z, buf, ring_send, ring_recv, sib_send, sib_recv):
        self.n, self.pos, self.core, self.z, self.buf = chips, pos, core, z, buf
        self.sems = ring_send, ring_recv, sib_send, sib_recv
        self.half = buf.shape[-1] // 2
        self.pending = []

    def chip(self, off):
        return snake(lax.rem(self.pos + off + self.n, self.n))

    def piece(self, off, core, h):
        return self.buf.at[self.chip(off) * 2 + core, :, pl.ds(h * self.half, self.half)]

    def hop(self, way, s, h, off):
        ref = self.piece(off, self.core, h)
        to = self.chip(1 if way == 0 else -1) * 2 + self.core
        return pltpu.make_async_remote_copy(
            ref, ref, self.sems[0].at[way, s - 1, h], self.sems[1].at[way, s - 1, h],
            device_id=(to, self.z), device_id_type=MESH)

    def cross(self, off, core, h):
        ref = self.piece(off, core, h)
        slot = off % self.n
        return pltpu.make_async_remote_copy(
            ref, ref, self.sems[2].at[slot, h], self.sems[3].at[slot, h],
            device_id=(self.chip(0) * 2 + 1 - self.core, self.z), device_id_type=MESH)

    def has(self, way, s, h):
        return s < self.n // 2 or (s == self.n // 2 and h == way)

    def go(self, copy):
        copy.start()
        self.pending.append(copy)

    def send_own(self, order):
        for h in order:
            for way in (0, 1):
                hh = h if way == 0 else order[1 - order.index(h)] if len(order) == 2 else h
                if self.has(way, 1, hh):
                    self.go(self.hop(way, 1, hh, 0))
        for h in order:
            self.go(self.cross(0, self.core, h))

    def arrive(self, way, s, h):
        off = -s if way == 0 else s
        self.hop(way, s, h, off).wait_recv()
        if self.has(way, s + 1, h):
            self.go(self.hop(way, s + 1, h, off))
        self.go(self.cross(off, self.core, h))

    def cross_wait(self, off, h):
        self.cross(off, 1 - self.core, h).wait_recv()

    def finish(self):
        for copy in self.pending:
            copy.wait_send()


def kernel(n_img, n_view, beta, images_ref, views_ref, out_ref,
           img, ihi, ilo, vws, vhi, vlo, hn, expo, phi, plo, stats, seen, num, rs_r, rs_l, rx_r, rx_l,
           mrow, mrx, res,
           in_sem, out_sem, ring_send, ring_recv, sib_send, sib_recv,
           oring_send, oring_recv, osib_send, osib_recv,
           v_send, v_recv, st_send, st_recv, r_send, r_recv, m_send, m_recv):
    i, z = lax.axis_index("img"), lax.axis_index("view")
    core, pos = lax.rem(i, 2), snake(i // 2)
    chips = n_img // 2
    rows = img.shape[1]
    part = vws.shape[1]
    feats = vws.shape[2]
    half = feats // 2

    own_img = pltpu.make_async_copy(images_ref, img.at[i], in_sem.at[0])
    own_vws = pltpu.make_async_copy(views_ref.at[pl.ds(i * part, part), :], vws.at[z], in_sem.at[1])
    own_img.start()
    own_vws.start()
    barrier = pltpu.get_barrier_semaphore()
    for d in range(1, n_img):
        pl.semaphore_signal(barrier, inc=1, device_id=(lax.rem(i + d, n_img), z), device_id_type=MESH)
    for d in range(1, n_view):
        pl.semaphore_signal(barrier, inc=1, device_id=(i, lax.rem(z + d, n_view)), device_id_type=MESH)
    own_img.wait()
    own_vws.wait()
    pl.semaphore_wait(barrier, n_img + n_view - 2)

    ring = Ring(chips, pos, core, z, img, ring_send, ring_recv, sib_send, sib_recv)
    ring.send_own((0, 1))

    def v_hop(way, j, block):
        ref = vws.at[block]
        to = z + 1 if way == 0 else z - 1
        return pltpu.make_async_remote_copy(
            ref, ref, v_send.at[way, j - 1], v_recv.at[way, j - 1], device_id=(i, to), device_id_type=MESH)

    def v_can(way):
        return z < n_view - 1 if way == 0 else z > 0

    for way in (0, 1):
        @pl.when(v_can(way))
        def _():
            v_hop(way, 1, z).start()

    def v_arrive(j):
        for way in (0, 1):
            block = z - j if way == 0 else z + j
            @pl.when(block >= 0 if way == 0 else block < n_view)
            def _():
                v_hop(way, j, block).wait_recv()

                @pl.when(v_can(way) if j < n_view - 1 else z < 0)
                def _():
                    v_hop(way, j + 1 if j < n_view - 1 else j, block).start()

    def prepare_views():
        current = vws[...].reshape(n_view * part, feats)
        hi, lo = split(current)
        vhi[...] = hi
        vlo[...] = lo
        hn[...] = jnp.broadcast_to(0.5 * jnp.sum(current * current, axis=1, keepdims=True), hn.shape)

    def score(off):
        c = ring.chip(off)
        x = img[pl.ds(2 * c, 2)].reshape(2 * rows, feats)
        hi, lo = split(x)
        ihi[c] = hi
        ilo[c] = lo
        s = dot_nt(vhi[...], hi) + dot_nt(vhi[...], lo) + dot_nt(vlo[...], hi)
        s = beta * (s - hn[:, 0:1])
        top = jnp.max(s, axis=0, keepdims=True)
        e = jnp.exp(s - top)
        expo[c] = e
        stats[c, 0:1, :] = top
        stats[c, 1:2, :] = jnp.sum(e, axis=0, keepdims=True)

    v_events = list(range(1, n_view))
    i_events = [(s, second) for s in range(1, chips // 2 + 1) for second in (0, 1)
                if s < chips // 2 or not second]
    order = []
    order += [("v", v) for v in v_events[:1]] + [("i", e) for e in i_events[:1]]
    order += [("v", v) for v in v_events[1:]] + [("i", e) for e in i_events[1:]]
    views_left = len(v_events)
    ready = [0]

    def flush():
        while ready:
            off = ready.pop(0)
            for h in (0, 1):
                ring.cross_wait(off, h)
            score(off)

    for kind, what in order:
        if kind == "v":
            v_arrive(what)
            views_left -= 1
            if views_left == 0:
                prepare_views()
                flush()
        else:
            s, second = what
            ring.arrive(0, s, second)
            ring.arrive(1, s, 1 - second)
            if s == chips // 2:
                ready += [s]
            elif second:
                ready += [-s, s]
            if views_left == 0:
                flush()

    sent = []
    for d in range(1, n_img):
        copy = pltpu.make_async_remote_copy(
            stats, seen.at[d - 1], st_send.at[d - 1], st_recv.at[d - 1],
            device_id=(lax.rem(i + d, n_img), z), device_id_type=MESH)
        copy.start()
        sent.append(copy)
    for copy in sent:
        copy.wait_recv()
    mass = jnp.zeros((n_view * part, 1), F32)
    for c in range(chips):
        mine = stats[c, 0:1, :]
        peak = mine
        for d in range(n_img - 1):
            peak = jnp.maximum(peak, seen[d, c, 0:1, :])
        factor = jnp.exp(mine - peak)
        total = stats[c, 1:2, :] * factor
        for d in range(n_img - 1):
            total = total + seen[d, c, 1:2, :] * jnp.exp(seen[d, c, 0:1, :] - peak)
        post = expo[c] * (factor / total)
        mass = mass + jnp.sum(post, axis=1, keepdims=True)
        hi, lo = split(post)
        phi[c] = hi
        plo[c] = lo

    eye = (lax.broadcasted_iota(jnp.int32, (part, 128), 0)
           == lax.broadcasted_iota(jnp.int32, (part, 128), 1))
    for b in range(n_view):
        col = mass[b * part:(b + 1) * part]
        row = jnp.sum(jnp.where(eye, col, 0.0), axis=0, keepdims=True)
        mrow[b] = jnp.broadcast_to(row, (8, 128))
    m_sent = []
    for d in range(1, n_view):
        to = lax.rem(z + d, n_view)
        copy = pltpu.make_async_remote_copy(
            mrow.at[to], mrx.at[d - 1], m_send.at[d - 1], m_recv.at[d - 1],
            device_id=(i, to), device_id_type=MESH)
        copy.start()
        m_sent.append(copy)

    def r_hop(way, b, h):
        src, dst = (rs_r, rx_r) if way == 0 else (rs_l, rx_l)
        to = z + 1 if way == 0 else z - 1
        return pltpu.make_async_remote_copy(
            src.at[h, b], dst.at[h, b], r_send.at[way, h, b], r_recv.at[way, h, b],
            device_id=(i, to), device_id_type=MESH)

    def from_start(way):
        return z == 0 if way == 0 else z == n_view - 1

    def passes(way, b):
        return z < b if way == 0 else z > b

    def blocks(way):
        return list(range(n_view - 1, 0, -1)) if way == 0 else list(range(n_view - 1))

    def numerators(h):
        total = jnp.zeros((n_view * part, half), F32)
        cols = pl.ds(h * half, half)
        for c in range(chips):
            total = total + (dot_nn(phi[c], ihi[c, :, cols]) + dot_nn(phi[c], ilo[c, :, cols])
                             + dot_nn(plo[c], ihi[c, :, cols]))
        num[h] = total.reshape(n_view, part, half)

    def reduce_start(h):
        for j in range(n_view - 1):
            for way in (0, 1):
                b = blocks(way)[j]

                @pl.when(from_start(way))
                def _():
                    src = rs_r if way == 0 else rs_l
                    src[h, b] = num[h, b]
                    r_hop(way, b, h).start()

    def reduce_pass(h):
        for j in range(n_view - 1):
            for way in (0, 1):
                b = blocks(way)[j]

                @pl.when(jnp.logical_and(jnp.logical_not(from_start(way)), passes(way, b)))
                def _():
                    src, got = (rs_r, rx_r) if way == 0 else (rs_l, rx_l)
                    r_hop(way, b, h).wait_recv()
                    src[h, b] = num[h, b] + got[h, b]
                    r_hop(way, b, h).start()

    out_ring = Ring(chips, pos, core, z, res, oring_send, oring_recv, osib_send, osib_recv)

    def last(h):
        for way in (0, 1):
            @pl.when(jnp.logical_not(from_start(way)))
            def _():
                got = rx_r if way == 0 else rx_l
                r_hop(way, z, h).wait_recv()
                num[h, z] = num[h, z] + got[h, z]

    def mass_total():
        for copy in m_sent:
            copy.wait_recv()
        row = mrow[z, 0:1, :]
        for d in range(n_view - 1):
            row = row + mrx[d, 0:1, :]
        return jnp.sum(jnp.where(eye, row, 0.0), axis=1, keepdims=True)

    for h in (0, 1):
        numerators(h)
        reduce_start(h)
    mass_all = None
    for h in (0, 1):
        reduce_pass(h)
        last(h)
        if h == 0:
            mass_all = mass_total()
        current = vws[z, :, pl.ds(h * half, half)]
        res[i, :, pl.ds(h * half, half)] = current + (num[h, z] - mass_all * current) / (mass_all + 1.0)
        out_ring.send_own((h,))

    stores = []

    def store(off, slot):
        c = out_ring.chip(off)
        copy = pltpu.make_async_copy(res.at[pl.ds(2 * c, 2)], out_ref.at[pl.ds(2 * c, 2)], out_sem.at[slot])
        copy.start()
        stores.append(copy)

    for s in range(1, chips // 2 + 1):
        for h in (0, 1):
            for way in (0, 1):
                if out_ring.has(way, s, h):
                    out_ring.arrive(way, s, h)
    for off in range(chips):
        for h in (0, 1):
            out_ring.cross_wait(off, h)
        store(off, off)

    ring.finish()
    out_ring.finish()
    for way in (0, 1):
        for j in range(1, n_view):
            block = z - (j - 1) if way == 0 else z + (j - 1)

            @pl.when(jnp.logical_and(v_can(way), block >= 0 if way == 0 else block < n_view))
            def _():
                v_hop(way, j, block).wait_send()
        for h in (0, 1):
            for b in blocks(way):
                @pl.when(passes(way, b))
                def _():
                    r_hop(way, b, h).wait_send()
    for copy in sent + m_sent:
        copy.wait_send()
    for copy in stores:
        copy.wait()


def on_device(n_img, n_view, images, views):
    inner, batch, feats = images.shape
    rows = inner * batch
    chips = n_img // 2
    part = views.shape[0] // n_img
    mine = n_view * part
    beta = 1.6 / math.sqrt(feats)
    half = feats // 2
    dma = pltpu.SemaphoreType.DMA
    vmem = pltpu.VMEM
    ring_sems = [dma((2, chips // 2, 2)), dma((2, chips // 2, 2)), dma((chips, 2)), dma((chips, 2))]
    out = pl.pallas_call(
        functools.partial(kernel, n_img, n_view, beta),
        out_shape=jax.ShapeDtypeStruct((n_img, part, feats), F32),
        in_specs=[pl.BlockSpec(memory_space=pl.ANY)] * 2,
        out_specs=pl.BlockSpec(memory_space=pl.ANY),
        scratch_shapes=[
            vmem((n_img, rows, feats), F32),
            vmem((chips, 2 * rows, feats), BF16),
            vmem((chips, 2 * rows, feats), BF16),
            vmem((n_view, part, feats), F32),
            vmem((mine, feats), BF16),
            vmem((mine, feats), BF16),
            vmem((mine, 128), F32),
            vmem((chips, mine, 2 * rows), F32),
            vmem((chips, mine, 2 * rows), BF16),
            vmem((chips, mine, 2 * rows), BF16),
            vmem((chips, 2, 2 * rows), F32),
            vmem((n_img - 1, chips, 2, 2 * rows), F32),
            vmem((2, n_view, part, half), F32),
            vmem((2, n_view, part, half), F32),
            vmem((2, n_view, part, half), F32),
            vmem((2, n_view, part, half), F32),
            vmem((2, n_view, part, half), F32),
            vmem((n_view, 8, 128), F32),
            vmem((n_view - 1, 8, 128), F32),
            vmem((n_img, part, feats), F32),
            dma((2,)), dma((chips,)),
        ] + ring_sems + ring_sems + [
            dma((2, n_view - 1)), dma((2, n_view - 1)),
            dma((n_img - 1,)), dma((n_img - 1,)),
            dma((2, 2, n_view)), dma((2, 2, n_view)),
            dma((n_view - 1,)), dma((n_view - 1,)),
        ],
        compiler_params=pltpu.CompilerParams(
            collective_id=0, has_side_effects=True, vmem_limit_bytes=48 * 1024 * 1024),
        cost_estimate=pl.CostEstimate(
            flops=12 * mine * n_img * rows * feats, bytes_accessed=16 * rows * feats, transcendentals=0),
    )(images.reshape(rows, feats), views)
    return out.reshape(n_img * part, feats)


def solution(mesh):
    placed = (P(None, ("img", "view"), None), P("view", None))
    return jax.shard_map(
        functools.partial(on_device, mesh.shape["img"], mesh.shape["view"]),
        mesh=mesh, in_specs=placed, out_specs=P("view", None), check_vma=False)
```

```python
import functools
import math

import jax
import jax.numpy as jnp
from jax import lax
from jax.experimental import pallas as pl
from jax.experimental.pallas import tpu as pltpu
from jax.sharding import PartitionSpec as P

MESH = pl.DeviceIdType.MESH
F32 = jnp.float32
BF16 = jnp.bfloat16
PIECES = 4


def snake(c):
    row, col = c // 2, c % 2
    return 2 * row + col + (row % 2) * (1 - 2 * col)


def split(x):
    hi = x.astype(BF16)
    return hi, (x - hi.astype(F32)).astype(BF16)


def dot_nt(a, b):
    return lax.dot_general(a, b, (((1,), (1,)), ((), ())), preferred_element_type=F32)


def dot_nn(a, b):
    return lax.dot_general(a, b, (((1,), (0,)), ((), ())), preferred_element_type=F32)


class Ring:
    def __init__(self, chips, pos, core, z, buf, parts, ring_send, ring_recv, sib_send, sib_recv):
        self.n, self.pos, self.core, self.z, self.buf = chips, pos, core, z, buf
        self.sems = ring_send, ring_recv, sib_send, sib_recv
        self.half = buf.shape[-1] // parts
        self.pending = []

    def chip(self, off):
        return snake(lax.rem(self.pos + off + self.n, self.n))

    def piece(self, off, core, h):
        return self.buf.at[self.chip(off) * 2 + core, :, pl.ds(h * self.half, self.half)]

    def hop(self, way, s, h, off):
        ref = self.piece(off, self.core, h)
        to = self.chip(1 if way == 0 else -1) * 2 + self.core
        return pltpu.make_async_remote_copy(
            ref, ref, self.sems[0].at[way, s - 1, h], self.sems[1].at[way, s - 1, h],
            device_id=(to, self.z), device_id_type=MESH)

    def cross(self, off, core, h):
        ref = self.piece(off, core, h)
        slot = off % self.n
        return pltpu.make_async_remote_copy(
            ref, ref, self.sems[2].at[slot, h], self.sems[3].at[slot, h],
            device_id=(self.chip(0) * 2 + 1 - self.core, self.z), device_id_type=MESH)

    def has(self, way, s, h):
        return s < self.n // 2 or (s == self.n // 2 and h % 2 == way)

    def go(self, copy):
        copy.start()
        self.pending.append(copy)

    def send_own(self, order):
        for h in order:
            for way in (0, 1):
                hh = h if way == 0 else order[1 - order.index(h)] if len(order) == 2 else h
                if self.has(way, 1, hh):
                    self.go(self.hop(way, 1, hh, 0))
        for h in order:
            self.go(self.cross(0, self.core, h))

    def arrive(self, way, s, h):
        off = -s if way == 0 else s
        self.hop(way, s, h, off).wait_recv()
        if self.has(way, s + 1, h):
            self.go(self.hop(way, s + 1, h, off))
        self.go(self.cross(off, self.core, h))

    def cross_wait(self, off, h):
        self.cross(off, 1 - self.core, h).wait_recv()

    def finish(self):
        for copy in self.pending:
            copy.wait_send()


def kernel(n_img, n_view, beta, images_ref, views_ref, out_ref,
           img, ihi, ilo, vws, vhi, vlo, hn, expo, phi, plo, stats, seen, num, rs_r, rs_l, rx_r, rx_l,
           mrow, mrx, res,
           in_sem, out_sem, ring_send, ring_recv, sib_send, sib_recv,
           oring_send, oring_recv, osib_send, osib_recv,
           v_send, v_recv, st_send, st_recv, r_send, r_recv, m_send, m_recv):
    i, z = lax.axis_index("img"), lax.axis_index("view")
    core, pos = lax.rem(i, 2), snake(i // 2)
    chips = n_img // 2
    rows = img.shape[1]
    part = vws.shape[1]
    feats = vws.shape[2]
    half = feats // PIECES

    own_img = pltpu.make_async_copy(images_ref, img.at[i], in_sem.at[0])
    own_vws = pltpu.make_async_copy(views_ref.at[pl.ds(i * part, part), :], vws.at[z], in_sem.at[1])
    own_img.start()
    own_vws.start()
    barrier = pltpu.get_barrier_semaphore()
    for d in range(1, n_img):
        pl.semaphore_signal(barrier, inc=1, device_id=(lax.rem(i + d, n_img), z), device_id_type=MESH)
    for d in range(1, n_view):
        pl.semaphore_signal(barrier, inc=1, device_id=(i, lax.rem(z + d, n_view)), device_id_type=MESH)
    own_img.wait()
    own_vws.wait()
    pl.semaphore_wait(barrier, n_img + n_view - 2)

    ring = Ring(chips, pos, core, z, img, 2, ring_send, ring_recv, sib_send, sib_recv)
    ring.send_own((0, 1))

    def v_hop(way, j, block):
        ref = vws.at[block]
        to = z + 1 if way == 0 else z - 1
        return pltpu.make_async_remote_copy(
            ref, ref, v_send.at[way, j - 1], v_recv.at[way, j - 1], device_id=(i, to), device_id_type=MESH)

    def v_can(way):
        return z < n_view - 1 if way == 0 else z > 0

    for way in (0, 1):
        @pl.when(v_can(way))
        def _():
            v_hop(way, 1, z).start()

    def v_arrive(j):
        for way in (0, 1):
            block = z - j if way == 0 else z + j
            @pl.when(block >= 0 if way == 0 else block < n_view)
            def _():
                v_hop(way, j, block).wait_recv()

                @pl.when(v_can(way) if j < n_view - 1 else z < 0)
                def _():
                    v_hop(way, j + 1 if j < n_view - 1 else j, block).start()

    def prepare_views():
        current = vws[...].reshape(n_view * part, feats)
        hi, lo = split(current)
        vhi[...] = hi
        vlo[...] = lo
        hn[...] = jnp.broadcast_to(0.5 * jnp.sum(current * current, axis=1, keepdims=True), hn.shape)

    def score(off):
        c = ring.chip(off)
        x = img[pl.ds(2 * c, 2)].reshape(2 * rows, feats)
        hi, lo = split(x)
        ihi[c] = hi
        ilo[c] = lo
        s = dot_nt(vhi[...], hi) + dot_nt(vhi[...], lo) + dot_nt(vlo[...], hi)
        s = beta * (s - hn[:, 0:1])
        top = jnp.max(s, axis=0, keepdims=True)
        e = jnp.exp(s - top)
        expo[c] = e
        stats[c, 0:1, :] = top
        stats[c, 1:2, :] = jnp.sum(e, axis=0, keepdims=True)

    v_events = list(range(1, n_view))
    i_events = [(s, second) for s in range(1, chips // 2 + 1) for second in (0, 1)
                if s < chips // 2 or not second]
    order = []
    order += [("v", v) for v in v_events[:1]] + [("i", e) for e in i_events[:1]]
    order += [("v", v) for v in v_events[1:]] + [("i", e) for e in i_events[1:]]
    views_left = len(v_events)
    ready = [0]

    def flush():
        while ready:
            off = ready.pop(0)
            for h in (0, 1):
                ring.cross_wait(off, h)
            score(off)

    for kind, what in order:
        if kind == "v":
            v_arrive(what)
            views_left -= 1
            if views_left == 0:
                prepare_views()
                flush()
        else:
            s, second = what
            ring.arrive(0, s, second)
            ring.arrive(1, s, 1 - second)
            if s == chips // 2:
                ready += [s]
            elif second:
                ready += [-s, s]
            if views_left == 0:
                flush()

    sent = []
    for d in range(1, n_img):
        copy = pltpu.make_async_remote_copy(
            stats, seen.at[d - 1], st_send.at[d - 1], st_recv.at[d - 1],
            device_id=(lax.rem(i + d, n_img), z), device_id_type=MESH)
        copy.start()
        sent.append(copy)
    for copy in sent:
        copy.wait_recv()
    mass = jnp.zeros((n_view * part, 1), F32)
    for c in range(chips):
        mine = stats[c, 0:1, :]
        peak = mine
        for d in range(n_img - 1):
            peak = jnp.maximum(peak, seen[d, c, 0:1, :])
        factor = jnp.exp(mine - peak)
        total = stats[c, 1:2, :] * factor
        for d in range(n_img - 1):
            total = total + seen[d, c, 1:2, :] * jnp.exp(seen[d, c, 0:1, :] - peak)
        post = expo[c] * (factor / total)
        mass = mass + jnp.sum(post, axis=1, keepdims=True)
        hi, lo = split(post)
        phi[c] = hi
        plo[c] = lo

    eye = (lax.broadcasted_iota(jnp.int32, (part, 128), 0)
           == lax.broadcasted_iota(jnp.int32, (part, 128), 1))
    for b in range(n_view):
        col = mass[b * part:(b + 1) * part]
        row = jnp.sum(jnp.where(eye, col, 0.0), axis=0, keepdims=True)
        mrow[b] = jnp.broadcast_to(row, (8, 128))
    m_sent = []
    for d in range(1, n_view):
        to = lax.rem(z + d, n_view)
        copy = pltpu.make_async_remote_copy(
            mrow.at[to], mrx.at[d - 1], m_send.at[d - 1], m_recv.at[d - 1],
            device_id=(i, to), device_id_type=MESH)
        copy.start()
        m_sent.append(copy)

    def r_hop(way, b, h):
        src, dst = (rs_r, rx_r) if way == 0 else (rs_l, rx_l)
        to = z + 1 if way == 0 else z - 1
        return pltpu.make_async_remote_copy(
            src.at[h, b], dst.at[h, b], r_send.at[way, h, b], r_recv.at[way, h, b],
            device_id=(i, to), device_id_type=MESH)

    def from_start(way):
        return z == 0 if way == 0 else z == n_view - 1

    def passes(way, b):
        return z < b if way == 0 else z > b

    def blocks(way):
        return list(range(n_view - 1, 0, -1)) if way == 0 else list(range(n_view - 1))

    def numerators(h):
        total = jnp.zeros((n_view * part, half), F32)
        cols = pl.ds(h * half, half)
        for c in range(chips):
            total = total + (dot_nn(phi[c], ihi[c, :, cols]) + dot_nn(phi[c], ilo[c, :, cols])
                             + dot_nn(plo[c], ihi[c, :, cols]))
        num[h] = total.reshape(n_view, part, half)

    def reduce_start(h):
        for j in range(n_view - 1):
            for way in (0, 1):
                b = blocks(way)[j]

                @pl.when(from_start(way))
                def _():
                    if h > 0:
                        r_hop(way, b, h - 1).wait_send()
                    src = rs_r if way == 0 else rs_l
                    src[h, b] = num[h, b]
                    r_hop(way, b, h).start()

    def reduce_pass(h):
        for j in range(n_view - 1):
            for way in (0, 1):
                b = blocks(way)[j]

                @pl.when(jnp.logical_and(jnp.logical_not(from_start(way)), passes(way, b)))
                def _():
                    src, got = (rs_r, rx_r) if way == 0 else (rs_l, rx_l)
                    r_hop(way, b, h).wait_recv()
                    src[h, b] = num[h, b] + got[h, b]
                    r_hop(way, b, h).start()

    out_ring = Ring(chips, pos, core, z, res, PIECES, oring_send, oring_recv, osib_send, osib_recv)

    def last(h):
        for way in (0, 1):
            @pl.when(jnp.logical_not(from_start(way)))
            def _():
                got = rx_r if way == 0 else rx_l
                r_hop(way, z, h).wait_recv()
                num[h, z] = num[h, z] + got[h, z]

    def mass_total():
        for copy in m_sent:
            copy.wait_recv()
        row = mrow[z, 0:1, :]
        for d in range(n_view - 1):
            row = row + mrx[d, 0:1, :]
        return jnp.sum(jnp.where(eye, row, 0.0), axis=1, keepdims=True)

    def gather(h):
        for s in range(1, chips // 2 + 1):
            for way in (0, 1):
                if out_ring.has(way, s, h):
                    out_ring.arrive(way, s, h)

    numerators(0)
    reduce_start(0)
    mass_all = None
    for h in range(PIECES):
        if h + 1 < PIECES:
            numerators(h + 1)
            reduce_start(h + 1)
        reduce_pass(h)
        last(h)
        if h == 0:
            mass_all = mass_total()
        current = vws[z, :, pl.ds(h * half, half)]
        res[i, :, pl.ds(h * half, half)] = current + (num[h, z] - mass_all * current) / (mass_all + 1.0)
        out_ring.send_own((h,))
        if h > 0:
            gather(h - 1)
    gather(PIECES - 1)

    stores = []
    for off in range(chips):
        for h in range(PIECES):
            out_ring.cross_wait(off, h)
        c = out_ring.chip(off)
        copy = pltpu.make_async_copy(res.at[pl.ds(2 * c, 2)], out_ref.at[pl.ds(2 * c, 2)], out_sem.at[off])
        copy.start()
        stores.append(copy)

    ring.finish()
    out_ring.finish()
    for way in (0, 1):
        for j in range(1, n_view):
            block = z - (j - 1) if way == 0 else z + (j - 1)

            @pl.when(jnp.logical_and(v_can(way), block >= 0 if way == 0 else block < n_view))
            def _():
                v_hop(way, j, block).wait_send()
        for h in range(PIECES):
            for b in blocks(way):
                going = passes(way, b)
                if h + 1 < PIECES:
                    going = jnp.logical_and(going, jnp.logical_not(from_start(way)))

                @pl.when(going)
                def _():
                    r_hop(way, b, h).wait_send()
    for copy in sent + m_sent:
        copy.wait_send()
    for copy in stores:
        copy.wait()


def on_device(n_img, n_view, images, views):
    inner, batch, feats = images.shape
    rows = inner * batch
    chips = n_img // 2
    part = views.shape[0] // n_img
    mine = n_view * part
    beta = 1.6 / math.sqrt(feats)
    half = feats // PIECES
    dma = pltpu.SemaphoreType.DMA
    vmem = pltpu.VMEM

    def ring_sems(parts):
        hops, crossings = (2, chips // 2, parts), (chips, parts)
        return [dma(hops), dma(hops), dma(crossings), dma(crossings)]

    out = pl.pallas_call(
        functools.partial(kernel, n_img, n_view, beta),
        out_shape=jax.ShapeDtypeStruct((n_img, part, feats), F32),
        in_specs=[pl.BlockSpec(memory_space=pl.ANY)] * 2,
        out_specs=pl.BlockSpec(memory_space=pl.ANY),
        scratch_shapes=[
            vmem((n_img, rows, feats), F32),
            vmem((chips, 2 * rows, feats), BF16),
            vmem((chips, 2 * rows, feats), BF16),
            vmem((n_view, part, feats), F32),
            vmem((mine, feats), BF16),
            vmem((mine, feats), BF16),
            vmem((mine, 128), F32),
            vmem((chips, mine, 2 * rows), F32),
            vmem((chips, mine, 2 * rows), BF16),
            vmem((chips, mine, 2 * rows), BF16),
            vmem((chips, 2, 2 * rows), F32),
            vmem((n_img - 1, chips, 2, 2 * rows), F32),
            vmem((PIECES, n_view, part, half), F32),
            vmem((PIECES, n_view, part, half), F32),
            vmem((PIECES, n_view, part, half), F32),
            vmem((PIECES, n_view, part, half), F32),
            vmem((PIECES, n_view, part, half), F32),
            vmem((n_view, 8, 128), F32),
            vmem((n_view - 1, 8, 128), F32),
            vmem((n_img, part, feats), F32),
            dma((2,)), dma((chips,)),
        ] + ring_sems(2) + ring_sems(PIECES) + [
            dma((2, n_view - 1)), dma((2, n_view - 1)),
            dma((n_img - 1,)), dma((n_img - 1,)),
            dma((2, PIECES, n_view)), dma((2, PIECES, n_view)),
            dma((n_view - 1,)), dma((n_view - 1,)),
        ],
        compiler_params=pltpu.CompilerParams(
            collective_id=0, has_side_effects=True, vmem_limit_bytes=60 * 1024 * 1024),
        cost_estimate=pl.CostEstimate(
            flops=12 * mine * n_img * rows * feats, bytes_accessed=16 * rows * feats, transcendentals=0),
    )(images.reshape(rows, feats), views)
    return out.reshape(n_img * part, feats)


def solution(mesh):
    placed = (P(None, ("img", "view"), None), P("view", None))
    return jax.shard_map(
        functools.partial(on_device, mesh.shape["img"], mesh.shape["view"]),
        mesh=mesh, in_specs=placed, out_specs=P("view", None), check_vma=False)
```

```python
import functools
import math

import jax
import jax.numpy as jnp
from jax import lax
from jax.experimental import pallas as pl
from jax.experimental.pallas import tpu as pltpu
from jax.sharding import PartitionSpec as P

MESH = pl.DeviceIdType.MESH
F32 = jnp.float32
BF16 = jnp.bfloat16


def snake(c):
    row, col = c // 2, c % 2
    return 2 * row + col + (row % 2) * (1 - 2 * col)


def split(x):
    hi = x.astype(BF16)
    return hi, (x - hi.astype(F32)).astype(BF16)


def dot_nt(a, b):
    return lax.dot_general(a, b, (((1,), (1,)), ((), ())), preferred_element_type=F32)


def dot_nn(a, b):
    return lax.dot_general(a, b, (((1,), (0,)), ((), ())), preferred_element_type=F32)


class Ring:
    def __init__(self, chips, pos, core, z, buf, ring_send, ring_recv, sib_send, sib_recv):
        self.n, self.pos, self.core, self.z, self.buf = chips, pos, core, z, buf
        self.sems = ring_send, ring_recv, sib_send, sib_recv
        self.half = buf.shape[-1] // 2
        self.pending = []

    def chip(self, off):
        return snake(lax.rem(self.pos + off + self.n, self.n))

    def piece(self, off, core, h):
        return self.buf.at[self.chip(off) * 2 + core, :, pl.ds(h * self.half, self.half)]

    def hop(self, way, s, h, off):
        ref = self.piece(off, self.core, h)
        to = self.chip(1 if way == 0 else -1) * 2 + self.core
        return pltpu.make_async_remote_copy(
            ref, ref, self.sems[0].at[way, s - 1, h], self.sems[1].at[way, s - 1, h],
            device_id=(to, self.z), device_id_type=MESH)

    def cross(self, off, core, h):
        ref = self.piece(off, core, h)
        slot = off % self.n
        return pltpu.make_async_remote_copy(
            ref, ref, self.sems[2].at[slot, h], self.sems[3].at[slot, h],
            device_id=(self.chip(0) * 2 + 1 - self.core, self.z), device_id_type=MESH)

    def has(self, way, s, h):
        return s < self.n // 2 or (s == self.n // 2 and h == way)

    def go(self, copy):
        copy.start()
        self.pending.append(copy)

    def send_own(self, order):
        for h in order:
            for way in (0, 1):
                hh = h if way == 0 else order[1 - order.index(h)] if len(order) == 2 else h
                if self.has(way, 1, hh):
                    self.go(self.hop(way, 1, hh, 0))
        for h in order:
            self.go(self.cross(0, self.core, h))

    def arrive(self, way, s, h):
        off = -s if way == 0 else s
        self.hop(way, s, h, off).wait_recv()
        if self.has(way, s + 1, h):
            self.go(self.hop(way, s + 1, h, off))
        self.go(self.cross(off, self.core, h))

    def direct(self, off, h, mine):
        ref = self.piece(0 if mine else -off, self.core, h)
        return pltpu.make_async_remote_copy(
            ref, ref, self.sems[0].at[off - 1, h], self.sems[1].at[off - 1, h],
            device_id=(self.chip(off) * 2 + self.core, self.z), device_id_type=MESH)

    def cross_wait(self, off, h):
        self.cross(off, 1 - self.core, h).wait_recv()

    def finish(self):
        for copy in self.pending:
            copy.wait_send()


def kernel(n_img, n_view, beta, images_ref, views_ref, out_ref,
           img, ihi, ilo, vws, vhi, vlo, hn, expo, phi, plo, stats, seen, num, rx,
           mrow, mrx, res,
           in_sem, out_sem, ring_send, ring_recv, sib_send, sib_recv,
           oring_send, oring_recv, osib_send, osib_recv,
           v_send, v_recv, st_send, st_recv, r_send, r_recv, m_send, m_recv):
    i, z = lax.axis_index("img"), lax.axis_index("view")
    core, pos = lax.rem(i, 2), snake(i // 2)
    chips = n_img // 2
    rows = img.shape[1]
    part = vws.shape[1]
    feats = vws.shape[2]
    half = feats // 2

    own_img = pltpu.make_async_copy(images_ref, img.at[i], in_sem.at[0])
    own_vws = pltpu.make_async_copy(views_ref.at[pl.ds(i * part, part), :], vws.at[z], in_sem.at[1])
    own_img.start()
    own_vws.start()
    barrier = pltpu.get_barrier_semaphore()
    for d in range(1, n_img):
        pl.semaphore_signal(barrier, inc=1, device_id=(lax.rem(i + d, n_img), z), device_id_type=MESH)
    for d in range(1, n_view):
        pl.semaphore_signal(barrier, inc=1, device_id=(i, lax.rem(z + d, n_view)), device_id_type=MESH)
    own_img.wait()
    own_vws.wait()
    pl.semaphore_wait(barrier, n_img + n_view - 2)

    ring = Ring(chips, pos, core, z, img, ring_send, ring_recv, sib_send, sib_recv)
    ring.send_own((0, 1))

    def v_hop(way, j, block):
        ref = vws.at[block]
        to = z + 1 if way == 0 else z - 1
        return pltpu.make_async_remote_copy(
            ref, ref, v_send.at[way, j - 1], v_recv.at[way, j - 1], device_id=(i, to), device_id_type=MESH)

    def v_can(way):
        return z < n_view - 1 if way == 0 else z > 0

    for way in (0, 1):
        @pl.when(v_can(way))
        def _():
            v_hop(way, 1, z).start()

    def v_arrive(j):
        for way in (0, 1):
            block = z - j if way == 0 else z + j
            @pl.when(block >= 0 if way == 0 else block < n_view)
            def _():
                v_hop(way, j, block).wait_recv()

                @pl.when(v_can(way) if j < n_view - 1 else z < 0)
                def _():
                    v_hop(way, j + 1 if j < n_view - 1 else j, block).start()

    def prepare_views():
        current = vws[...].reshape(n_view * part, feats)
        hi, lo = split(current)
        vhi[...] = hi
        vlo[...] = lo
        hn[...] = jnp.broadcast_to(0.5 * jnp.sum(current * current, axis=1, keepdims=True), hn.shape)

    def score(off):
        c = ring.chip(off)
        x = img[pl.ds(2 * c, 2)].reshape(2 * rows, feats)
        hi, lo = split(x)
        ihi[c] = hi
        ilo[c] = lo
        s = dot_nt(vhi[...], hi) + dot_nt(vhi[...], lo) + dot_nt(vlo[...], hi)
        s = beta * (s - hn[:, 0:1])
        top = jnp.max(s, axis=0, keepdims=True)
        e = jnp.exp(s - top)
        expo[c] = e
        stats[c, 0:1, :] = top
        stats[c, 1:2, :] = jnp.sum(e, axis=0, keepdims=True)

    v_events = list(range(1, n_view))
    i_events = [(s, second) for s in range(1, chips // 2 + 1) for second in (0, 1)
                if s < chips // 2 or not second]
    order = []
    order += [("v", v) for v in v_events[:2]] + [("i", e) for e in i_events[:1]]
    order += [("v", v) for v in v_events[2:]] + [("i", e) for e in i_events[1:]]
    views_left = len(v_events)
    ready = [0]

    def flush():
        while ready:
            off = ready.pop(0)
            for h in (0, 1):
                ring.cross_wait(off, h)
            score(off)

    for kind, what in order:
        if kind == "v":
            v_arrive(what)
            views_left -= 1
            if views_left == 0:
                prepare_views()
                flush()
        else:
            s, second = what
            ring.arrive(0, s, second)
            ring.arrive(1, s, 1 - second)
            if s == chips // 2:
                ready += [s]
            elif second:
                ready += [-s, s]
            if views_left == 0:
                flush()

    sent = []
    for d in range(1, n_img):
        copy = pltpu.make_async_remote_copy(
            stats, seen.at[d - 1], st_send.at[d - 1], st_recv.at[d - 1],
            device_id=(lax.rem(i + d, n_img), z), device_id_type=MESH)
        copy.start()
        sent.append(copy)
    for copy in sent:
        copy.wait_recv()
    mass = jnp.zeros((n_view * part, 1), F32)
    for c in range(chips):
        mine = stats[c, 0:1, :]
        peak = mine
        for d in range(n_img - 1):
            peak = jnp.maximum(peak, seen[d, c, 0:1, :])
        factor = jnp.exp(mine - peak)
        total = stats[c, 1:2, :] * factor
        for d in range(n_img - 1):
            total = total + seen[d, c, 1:2, :] * jnp.exp(seen[d, c, 0:1, :] - peak)
        post = expo[c] * (factor / total)
        mass = mass + jnp.sum(post, axis=1, keepdims=True)
        hi, lo = split(post)
        phi[c] = hi
        plo[c] = lo

    eye = (lax.broadcasted_iota(jnp.int32, (part, 128), 0)
           == lax.broadcasted_iota(jnp.int32, (part, 128), 1))
    for b in range(n_view):
        col = mass[b * part:(b + 1) * part]
        row = jnp.sum(jnp.where(eye, col, 0.0), axis=0, keepdims=True)
        mrow[b] = jnp.broadcast_to(row, (8, 128))
    m_sent = []
    for d in range(1, n_view):
        to = lax.rem(z + d, n_view)
        copy = pltpu.make_async_remote_copy(
            mrow.at[to], mrx.at[d - 1], m_send.at[d - 1], m_recv.at[d - 1],
            device_id=(i, to), device_id_type=MESH)
        copy.start()
        m_sent.append(copy)

    r_sent = []

    def numerators(h):
        total = jnp.zeros((n_view * part, half), F32)
        cols = pl.ds(h * half, half)
        for c in range(chips):
            total = total + (dot_nn(phi[c], ihi[c, :, cols]) + dot_nn(phi[c], ilo[c, :, cols])
                             + dot_nn(plo[c], ihi[c, :, cols]))
        num[h] = total.reshape(n_view, part, half)
        for d in range(1, n_view):
            to = lax.rem(z + d, n_view)
            copy = pltpu.make_async_remote_copy(
                num.at[h, to], rx.at[h, d - 1], r_send.at[h, d - 1], r_recv.at[h, d - 1],
                device_id=(i, to), device_id_type=MESH)
            copy.start()
            r_sent.append(copy)

    out_ring = Ring(chips, pos, core, z, res, oring_send, oring_recv, osib_send, osib_recv)

    def summed(h):
        total = num[h, z]
        for d in range(n_view - 1):
            r_sent[h * (n_view - 1) + d].wait_recv()
            total = total + rx[h, d]
        return total

    def mass_total():
        for copy in m_sent:
            copy.wait_recv()
        row = mrow[z, 0:1, :]
        for d in range(n_view - 1):
            row = row + mrx[d, 0:1, :]
        return jnp.sum(jnp.where(eye, row, 0.0), axis=1, keepdims=True)

    for h in (0, 1):
        numerators(h)
    mass_all = mass_total()
    for h in (0, 1):
        current = vws[z, :, pl.ds(h * half, half)]
        res[i, :, pl.ds(h * half, half)] = current + (summed(h) - mass_all * current) / (mass_all + 1.0)
        for off in range(1, chips):
            out_ring.go(out_ring.direct(off, h, True))
        out_ring.go(out_ring.cross(0, core, h))

    for h in (0, 1):
        for off in range(1, chips):
            out_ring.direct(off, h, False).wait_recv()
            out_ring.go(out_ring.cross(-off, core, h))

    stores = []
    for off in range(chips):
        for h in (0, 1):
            out_ring.cross_wait(-off, h)
        c = out_ring.chip(-off)
        copy = pltpu.make_async_copy(res.at[pl.ds(2 * c, 2)], out_ref.at[pl.ds(2 * c, 2)], out_sem.at[off])
        copy.start()
        stores.append(copy)

    ring.finish()
    out_ring.finish()
    for way in (0, 1):
        for j in range(1, n_view):
            block = z - (j - 1) if way == 0 else z + (j - 1)

            @pl.when(jnp.logical_and(v_can(way), block >= 0 if way == 0 else block < n_view))
            def _():
                v_hop(way, j, block).wait_send()
    for copy in sent + m_sent + r_sent:
        copy.wait_send()
    for copy in stores:
        copy.wait()


def on_device(n_img, n_view, images, views):
    inner, batch, feats = images.shape
    rows = inner * batch
    chips = n_img // 2
    part = views.shape[0] // n_img
    mine = n_view * part
    beta = 1.6 / math.sqrt(feats)
    half = feats // 2
    dma = pltpu.SemaphoreType.DMA
    vmem = pltpu.VMEM
    ring_sems = [dma((2, chips // 2, 2)), dma((2, chips // 2, 2)), dma((chips, 2)), dma((chips, 2))]
    out = pl.pallas_call(
        functools.partial(kernel, n_img, n_view, beta),
        out_shape=jax.ShapeDtypeStruct((n_img, part, feats), F32),
        in_specs=[pl.BlockSpec(memory_space=pltpu.HBM)] * 2,
        out_specs=pl.BlockSpec(memory_space=pl.ANY),
        scratch_shapes=[
            vmem((n_img, rows, feats), F32),
            vmem((chips, 2 * rows, feats), BF16),
            vmem((chips, 2 * rows, feats), BF16),
            vmem((n_view, part, feats), F32),
            vmem((mine, feats), BF16),
            vmem((mine, feats), BF16),
            vmem((mine, 128), F32),
            vmem((chips, mine, 2 * rows), F32),
            vmem((chips, mine, 2 * rows), BF16),
            vmem((chips, mine, 2 * rows), BF16),
            vmem((chips, 2, 2 * rows), F32),
            vmem((n_img - 1, chips, 2, 2 * rows), F32),
            vmem((2, n_view, part, half), F32),
            vmem((2, n_view - 1, part, half), F32),
            vmem((n_view, 8, 128), F32),
            vmem((n_view - 1, 8, 128), F32),
            vmem((n_img, part, feats), F32),
            dma((2,)), dma((chips,)),
        ] + ring_sems + [dma((chips - 1, 2)), dma((chips - 1, 2)), dma((chips, 2)), dma((chips, 2))] + [
            dma((2, n_view - 1)), dma((2, n_view - 1)),
            dma((n_img - 1,)), dma((n_img - 1,)),
            dma((2, n_view - 1)), dma((2, n_view - 1)),
            dma((n_view - 1,)), dma((n_view - 1,)),
        ],
        compiler_params=pltpu.CompilerParams(
            collective_id=0, has_side_effects=True, vmem_limit_bytes=48 * 1024 * 1024),
        cost_estimate=pl.CostEstimate(
            flops=12 * mine * n_img * rows * feats, bytes_accessed=16 * rows * feats, transcendentals=0),
    )(images.reshape(rows, feats), views)
    return out.reshape(n_img * part, feats)


def solution(mesh):
    placed = (P(None, ("img", "view"), None), P("view", None))
    return jax.shard_map(
        functools.partial(on_device, mesh.shape["img"], mesh.shape["view"]),
        mesh=mesh, in_specs=placed, out_specs=P("view", None), check_vma=False)
```

```python
import functools
import math

import jax
import jax.numpy as jnp
from jax import lax
from jax.experimental import pallas as pl
from jax.experimental.pallas import tpu as pltpu
from jax.sharding import PartitionSpec as P

MESH = pl.DeviceIdType.MESH
F32 = jnp.float32
BF16 = jnp.bfloat16


def snake(c):
    row, col = c // 2, c % 2
    return 2 * row + col + (row % 2) * (1 - 2 * col)


def split(x):
    hi = x.astype(BF16)
    return hi, (x - hi.astype(F32)).astype(BF16)


def dot_nt(a, b):
    return lax.dot_general(a, b, (((1,), (1,)), ((), ())), preferred_element_type=F32)


def dot_nn(a, b):
    return lax.dot_general(a, b, (((1,), (0,)), ((), ())), preferred_element_type=F32)


class Ring:
    def __init__(self, chips, pos, core, z, buf, ring_send, ring_recv, sib_send, sib_recv):
        self.n, self.pos, self.core, self.z, self.buf = chips, pos, core, z, buf
        self.sems = ring_send, ring_recv, sib_send, sib_recv
        self.half = buf.shape[-1] // 2
        self.pending = []

    def chip(self, off):
        return snake(lax.rem(self.pos + off + self.n, self.n))

    def piece(self, off, core, h):
        return self.buf.at[self.chip(off) * 2 + core, :, pl.ds(h * self.half, self.half)]

    def hop(self, way, s, h, off):
        ref = self.piece(off, self.core, h)
        to = self.chip(1 if way == 0 else -1) * 2 + self.core
        return pltpu.make_async_remote_copy(
            ref, ref, self.sems[0].at[way, s - 1, h], self.sems[1].at[way, s - 1, h],
            device_id=(to, self.z), device_id_type=MESH)

    def cross(self, off, core, h):
        ref = self.piece(off, core, h)
        slot = off % self.n
        return pltpu.make_async_remote_copy(
            ref, ref, self.sems[2].at[slot, h], self.sems[3].at[slot, h],
            device_id=(self.chip(0) * 2 + 1 - self.core, self.z), device_id_type=MESH)

    def has(self, way, s, h):
        return s < self.n // 2 or (s == self.n // 2 and h == way)

    def go(self, copy):
        copy.start()
        self.pending.append(copy)

    def send_own(self, order):
        for h in order:
            for way in (0, 1):
                hh = h if way == 0 else order[1 - order.index(h)] if len(order) == 2 else h
                if self.has(way, 1, hh):
                    self.go(self.hop(way, 1, hh, 0))
        for h in order:
            self.go(self.cross(0, self.core, h))

    def arrive(self, way, s, h):
        off = -s if way == 0 else s
        self.hop(way, s, h, off).wait_recv()
        if self.has(way, s + 1, h):
            self.go(self.hop(way, s + 1, h, off))
        self.go(self.cross(off, self.core, h))

    def direct(self, off, h, mine):
        ref = self.piece(0 if mine else -off, self.core, h)
        return pltpu.make_async_remote_copy(
            ref, ref, self.sems[0].at[off - 1, h], self.sems[1].at[off - 1, h],
            device_id=(self.chip(off) * 2 + self.core, self.z), device_id_type=MESH)

    def cross_wait(self, off, h):
        self.cross(off, 1 - self.core, h).wait_recv()

    def finish(self):
        for copy in self.pending:
            copy.wait_send()


def kernel(n_img, n_view, beta, images_ref, views_ref, out_ref,
           img, ihi, ilo, vws, vhi, vlo, hn, expo, phi, plo, stats, seen, num, rx,
           mrow, mrx, res,
           in_sem, out_sem, ring_send, ring_recv, sib_send, sib_recv,
           oring_send, oring_recv, osib_send, osib_recv,
           v_send, v_recv, st_send, st_recv, r_send, r_recv, m_send, m_recv):
    i, z = lax.axis_index("img"), lax.axis_index("view")
    core, pos = lax.rem(i, 2), snake(i // 2)
    chips = n_img // 2
    rows = img.shape[1]
    part = vws.shape[1]
    feats = vws.shape[2]
    half = feats // 2

    own_img = pltpu.make_async_copy(images_ref, img.at[i], in_sem.at[0])
    own_vws = pltpu.make_async_copy(views_ref.at[pl.ds(i * part, part), :], vws.at[z], in_sem.at[1])
    own_img.start()
    own_vws.start()
    barrier = pltpu.get_barrier_semaphore()
    for d in range(1, n_img):
        pl.semaphore_signal(barrier, inc=1, device_id=(lax.rem(i + d, n_img), z), device_id_type=MESH)
    for d in range(1, n_view):
        pl.semaphore_signal(barrier, inc=1, device_id=(i, lax.rem(z + d, n_view)), device_id_type=MESH)
    own_img.wait()
    own_vws.wait()
    pl.semaphore_wait(barrier, n_img + n_view - 2)

    ring = Ring(chips, pos, core, z, img, ring_send, ring_recv, sib_send, sib_recv)
    ring.send_own((0, 1))

    def v_hop(way, j, block, h):
        ref = vws.at[block, :, pl.ds(h * half, half)]
        to = z + 1 if way == 0 else z - 1
        return pltpu.make_async_remote_copy(
            ref, ref, v_send.at[way, j - 1, h], v_recv.at[way, j - 1, h], device_id=(i, to), device_id_type=MESH)

    def v_can(way):
        return z < n_view - 1 if way == 0 else z > 0

    for h in (0, 1):
        for way in (0, 1):
            @pl.when(v_can(way))
            def _():
                v_hop(way, 1, z, h).start()

    def prepare_block(block):
        current = vws[block]
        hi, lo = split(current)
        at = pl.ds(pl.multiple_of(block * part, part), part)
        vhi[at, :] = hi
        vlo[at, :] = lo
        hn[at, :] = jnp.broadcast_to(0.5 * jnp.sum(current * current, axis=1, keepdims=True), (part, 128))

    def v_arrive(j, h):
        for way in (0, 1):
            block = z - j if way == 0 else z + j
            @pl.when(block >= 0 if way == 0 else block < n_view)
            def _():
                v_hop(way, j, block, h).wait_recv()
                if j < n_view - 1:
                    @pl.when(v_can(way))
                    def _():
                        v_hop(way, j + 1, block, h).start()
                if h == 1:
                    prepare_block(block)

    def prepare_images(off):
        c = ring.chip(off)
        for h in (0, 1):
            ring.cross_wait(off, h)
        hi, lo = split(img[pl.ds(2 * c, 2)].reshape(2 * rows, feats))
        ihi[c] = hi
        ilo[c] = lo

    prepare_block(z)

    def score(off):
        c = ring.chip(off)
        s = dot_nt(vhi[...], ihi[c]) + dot_nt(vhi[...], ilo[c]) + dot_nt(vlo[...], ihi[c])
        s = beta * (s - hn[:, 0:1])
        top = jnp.max(s, axis=0, keepdims=True)
        e = jnp.exp(s - top)
        expo[c] = e
        stats[c, 0:1, :] = top
        stats[c, 1:2, :] = jnp.sum(e, axis=0, keepdims=True)

    v_events = [(j, h) for j in range(1, n_view) for h in (0, 1)]
    i_events = [(s, second) for s in range(1, chips // 2 + 1) for second in (0, 1)
                if s < chips // 2 or not second]
    order = []
    order += [("v", v) for v in v_events[:4]] + [("i", e) for e in i_events[:1]]
    order += [("v", v) for v in v_events[4:]] + [("i", e) for e in i_events[1:]]
    views_left = len(v_events)
    ready = [0]

    def flush():
        while ready:
            off = ready.pop(0)
            if off:
                prepare_images(off)
            score(off)

    for kind, what in order:
        if kind == "v":
            v_arrive(*what)
            if views_left == len(v_events):
                prepare_images(0)
            views_left -= 1
            if views_left == 0:
                flush()
        else:
            s, second = what
            ring.arrive(0, s, second)
            ring.arrive(1, s, 1 - second)
            if s == chips // 2:
                ready += [s]
            elif second:
                ready += [-s, s]
            if views_left == 0:
                flush()

    sent = []
    for d in range(1, n_img):
        copy = pltpu.make_async_remote_copy(
            stats, seen.at[d - 1], st_send.at[d - 1], st_recv.at[d - 1],
            device_id=(lax.rem(i + d, n_img), z), device_id_type=MESH)
        copy.start()
        sent.append(copy)
    for copy in sent:
        copy.wait_recv()
    mass = jnp.zeros((n_view * part, 1), F32)
    for c in range(chips):
        mine = stats[c, 0:1, :]
        peak = mine
        for d in range(n_img - 1):
            peak = jnp.maximum(peak, seen[d, c, 0:1, :])
        factor = jnp.exp(mine - peak)
        total = stats[c, 1:2, :] * factor
        for d in range(n_img - 1):
            total = total + seen[d, c, 1:2, :] * jnp.exp(seen[d, c, 0:1, :] - peak)
        post = expo[c] * (factor / total)
        mass = mass + jnp.sum(post, axis=1, keepdims=True)
        hi, lo = split(post)
        phi[c] = hi
        plo[c] = lo

    eye = (lax.broadcasted_iota(jnp.int32, (part, 128), 0)
           == lax.broadcasted_iota(jnp.int32, (part, 128), 1))
    for b in range(n_view):
        col = mass[b * part:(b + 1) * part]
        row = jnp.sum(jnp.where(eye, col, 0.0), axis=0, keepdims=True)
        mrow[b] = jnp.broadcast_to(row, (8, 128))
    m_sent = []
    for d in range(1, n_view):
        to = lax.rem(z + d, n_view)
        copy = pltpu.make_async_remote_copy(
            mrow.at[to], mrx.at[d - 1], m_send.at[d - 1], m_recv.at[d - 1],
            device_id=(i, to), device_id_type=MESH)
        copy.start()
        m_sent.append(copy)

    r_sent = []

    def numerators(h):
        total = jnp.zeros((n_view * part, half), F32)
        cols = pl.ds(h * half, half)
        for c in range(chips):
            total = total + (dot_nn(phi[c], ihi[c, :, cols]) + dot_nn(phi[c], ilo[c, :, cols])
                             + dot_nn(plo[c], ihi[c, :, cols]))
        num[h] = total.reshape(n_view, part, half)
        for d in range(1, n_view):
            to = lax.rem(z + d, n_view)
            copy = pltpu.make_async_remote_copy(
                num.at[h, to], rx.at[h, d - 1], r_send.at[h, d - 1], r_recv.at[h, d - 1],
                device_id=(i, to), device_id_type=MESH)
            copy.start()
            r_sent.append(copy)

    out_ring = Ring(chips, pos, core, z, res, oring_send, oring_recv, osib_send, osib_recv)

    def summed(h):
        total = num[h, z]
        for d in range(n_view - 1):
            r_sent[h * (n_view - 1) + d].wait_recv()
            total = total + rx[h, d]
        return total

    def mass_total():
        for copy in m_sent:
            copy.wait_recv()
        row = mrow[z, 0:1, :]
        for d in range(n_view - 1):
            row = row + mrx[d, 0:1, :]
        return jnp.sum(jnp.where(eye, row, 0.0), axis=1, keepdims=True)

    for h in (0, 1):
        numerators(h)
    mass_all = mass_total()
    for h in (0, 1):
        current = vws[z, :, pl.ds(h * half, half)]
        res[i, :, pl.ds(h * half, half)] = current + (summed(h) - mass_all * current) / (mass_all + 1.0)
        for off in range(1, chips):
            out_ring.go(out_ring.direct(off, h, True))
        out_ring.go(out_ring.cross(0, core, h))

    for h in (0, 1):
        for off in range(1, chips):
            out_ring.direct(off, h, False).wait_recv()
            out_ring.go(out_ring.cross(-off, core, h))

    stores = []
    for off in range(chips):
        for h in (0, 1):
            out_ring.cross_wait(-off, h)
        c = out_ring.chip(-off)
        copy = pltpu.make_async_copy(res.at[pl.ds(2 * c, 2)], out_ref.at[pl.ds(2 * c, 2)], out_sem.at[off])
        copy.start()
        stores.append(copy)

    ring.finish()
    out_ring.finish()
    for way in (0, 1):
        for j in range(1, n_view):
            block = z - (j - 1) if way == 0 else z + (j - 1)

            @pl.when(jnp.logical_and(v_can(way), block >= 0 if way == 0 else block < n_view))
            def _():
                for h in (0, 1):
                    v_hop(way, j, block, h).wait_send()
    for copy in sent + m_sent + r_sent:
        copy.wait_send()
    for copy in stores:
        copy.wait()


def on_device(n_img, n_view, images, views):
    inner, batch, feats = images.shape
    rows = inner * batch
    chips = n_img // 2
    part = views.shape[0] // n_img
    mine = n_view * part
    beta = 1.6 / math.sqrt(feats)
    half = feats // 2
    dma = pltpu.SemaphoreType.DMA
    vmem = pltpu.VMEM
    ring_sems = [dma((2, chips // 2, 2)), dma((2, chips // 2, 2)), dma((chips, 2)), dma((chips, 2))]
    out = pl.pallas_call(
        functools.partial(kernel, n_img, n_view, beta),
        out_shape=jax.ShapeDtypeStruct((n_img, part, feats), F32),
        in_specs=[pl.BlockSpec(memory_space=pl.ANY)] * 2,
        out_specs=pl.BlockSpec(memory_space=pl.ANY),
        scratch_shapes=[
            vmem((n_img, rows, feats), F32),
            vmem((chips, 2 * rows, feats), BF16),
            vmem((chips, 2 * rows, feats), BF16),
            vmem((n_view, part, feats), F32),
            vmem((mine, feats), BF16),
            vmem((mine, feats), BF16),
            vmem((mine, 128), F32),
            vmem((chips, mine, 2 * rows), F32),
            vmem((chips, mine, 2 * rows), BF16),
            vmem((chips, mine, 2 * rows), BF16),
            vmem((chips, 2, 2 * rows), F32),
            vmem((n_img - 1, chips, 2, 2 * rows), F32),
            vmem((2, n_view, part, half), F32),
            vmem((2, n_view - 1, part, half), F32),
            vmem((n_view, 8, 128), F32),
            vmem((n_view - 1, 8, 128), F32),
            vmem((n_img, part, feats), F32),
            dma((2,)), dma((chips,)),
        ] + ring_sems + [dma((chips - 1, 2)), dma((chips - 1, 2)), dma((chips, 2)), dma((chips, 2))] + [
            dma((2, n_view - 1, 2)), dma((2, n_view - 1, 2)),
            dma((n_img - 1,)), dma((n_img - 1,)),
            dma((2, n_view - 1)), dma((2, n_view - 1)),
            dma((n_view - 1,)), dma((n_view - 1,)),
        ],
        compiler_params=pltpu.CompilerParams(
            collective_id=0, has_side_effects=True, vmem_limit_bytes=51 * 1024 * 1024),
        cost_estimate=pl.CostEstimate(
            flops=12 * mine * n_img * rows * feats, bytes_accessed=16 * rows * feats, transcendentals=0),
    )(images.reshape(rows, feats), views)
    return out.reshape(n_img * part, feats)


def solution(mesh):
    placed = (P(None, ("img", "view"), None), P("view", None))
    return jax.shard_map(
        functools.partial(on_device, mesh.shape["img"], mesh.shape["view"]),
        mesh=mesh, in_specs=placed, out_specs=P("view", None), check_vma=False)
```

```python
import functools
import math

import jax
import jax.numpy as jnp
from jax import lax
from jax.experimental import pallas as pl
from jax.experimental.pallas import tpu as pltpu
from jax.sharding import PartitionSpec as P

MESH = pl.DeviceIdType.MESH
F32 = jnp.float32
BF16 = jnp.bfloat16
PIECES = 4


def snake(c):
    row, col = c // 2, c % 2
    return 2 * row + col + (row % 2) * (1 - 2 * col)


def split(x):
    hi = x.astype(BF16)
    return hi, (x - hi.astype(F32)).astype(BF16)


def dot_nt(a, b):
    return lax.dot_general(a, b, (((1,), (1,)), ((), ())), preferred_element_type=F32)


def dot_nn(a, b):
    return lax.dot_general(a, b, (((1,), (0,)), ((), ())), preferred_element_type=F32)


class Ring:
    def __init__(self, chips, pos, core, z, buf, parts, ring_send, ring_recv, sib_send, sib_recv):
        self.n, self.pos, self.core, self.z, self.buf = chips, pos, core, z, buf
        self.sems = ring_send, ring_recv, sib_send, sib_recv
        self.half = buf.shape[-1] // parts
        self.pending = []

    def chip(self, off):
        return snake(lax.rem(self.pos + off + self.n, self.n))

    def piece(self, off, core, h):
        return self.buf.at[self.chip(off) * 2 + core, :, pl.ds(h * self.half, self.half)]

    def hop(self, way, s, h, off):
        ref = self.piece(off, self.core, h)
        to = self.chip(1 if way == 0 else -1) * 2 + self.core
        return pltpu.make_async_remote_copy(
            ref, ref, self.sems[0].at[way, s - 1, h], self.sems[1].at[way, s - 1, h],
            device_id=(to, self.z), device_id_type=MESH)

    def cross(self, off, core, h):
        ref = self.piece(off, core, h)
        slot = off % self.n
        return pltpu.make_async_remote_copy(
            ref, ref, self.sems[2].at[slot, h], self.sems[3].at[slot, h],
            device_id=(self.chip(0) * 2 + 1 - self.core, self.z), device_id_type=MESH)

    def has(self, way, s, h):
        return s < self.n // 2 or (s == self.n // 2 and h == way)

    def go(self, copy):
        copy.start()
        self.pending.append(copy)

    def send_own(self, order):
        for h in order:
            for way in (0, 1):
                hh = h if way == 0 else order[1 - order.index(h)] if len(order) == 2 else h
                if self.has(way, 1, hh):
                    self.go(self.hop(way, 1, hh, 0))
        for h in order:
            self.go(self.cross(0, self.core, h))

    def arrive(self, way, s, h):
        off = -s if way == 0 else s
        self.hop(way, s, h, off).wait_recv()
        if self.has(way, s + 1, h):
            self.go(self.hop(way, s + 1, h, off))
        self.go(self.cross(off, self.core, h))

    def direct(self, off, h, mine):
        ref = self.piece(0 if mine else -off, self.core, h)
        return pltpu.make_async_remote_copy(
            ref, ref, self.sems[0].at[off - 1, h], self.sems[1].at[off - 1, h],
            device_id=(self.chip(off) * 2 + self.core, self.z), device_id_type=MESH)

    def cross_wait(self, off, h):
        self.cross(off, 1 - self.core, h).wait_recv()

    def finish(self):
        for copy in self.pending:
            copy.wait_send()


def kernel(n_img, n_view, beta, images_ref, views_ref, out_ref,
           img, ihi, ilo, vws, vhi, vlo, hn, expo, phi, plo, stats, seen, num, rx,
           mrow, mrx, res,
           in_sem, out_sem, ring_send, ring_recv, sib_send, sib_recv,
           oring_send, oring_recv, osib_send, osib_recv,
           v_send, v_recv, st_send, st_recv, r_send, r_recv, m_send, m_recv):
    i, z = lax.axis_index("img"), lax.axis_index("view")
    core, pos = lax.rem(i, 2), snake(i // 2)
    chips = n_img // 2
    rows = img.shape[1]
    part = vws.shape[1]
    feats = vws.shape[2]
    half = feats // 2
    width = feats // PIECES

    own_img = pltpu.make_async_copy(images_ref, img.at[i], in_sem.at[0])
    own_vws = pltpu.make_async_copy(views_ref.at[pl.ds(i * part, part), :], vws.at[z], in_sem.at[1])
    own_img.start()
    own_vws.start()
    barrier = pltpu.get_barrier_semaphore()
    for d in range(1, n_img):
        pl.semaphore_signal(barrier, inc=1, device_id=(lax.rem(i + d, n_img), z), device_id_type=MESH)
    for d in range(1, n_view):
        pl.semaphore_signal(barrier, inc=1, device_id=(i, lax.rem(z + d, n_view)), device_id_type=MESH)
    own_img.wait()
    own_vws.wait()
    pl.semaphore_wait(barrier, n_img + n_view - 2)

    ring = Ring(chips, pos, core, z, img, 2, ring_send, ring_recv, sib_send, sib_recv)
    ring.send_own((0, 1))

    def v_hop(way, j, block, h):
        ref = vws.at[block, :, pl.ds(h * half, half)]
        to = z + 1 if way == 0 else z - 1
        return pltpu.make_async_remote_copy(
            ref, ref, v_send.at[way, j - 1, h], v_recv.at[way, j - 1, h], device_id=(i, to), device_id_type=MESH)

    def v_can(way):
        return z < n_view - 1 if way == 0 else z > 0

    for h in (0, 1):
        for way in (0, 1):
            @pl.when(v_can(way))
            def _():
                v_hop(way, 1, z, h).start()

    def prepare_block(block):
        current = vws[block]
        hi, lo = split(current)
        at = pl.ds(pl.multiple_of(block * part, part), part)
        vhi[at, :] = hi
        vlo[at, :] = lo
        hn[at, :] = jnp.broadcast_to(0.5 * jnp.sum(current * current, axis=1, keepdims=True), (part, 128))

    def v_arrive(j, h):
        for way in (0, 1):
            block = z - j if way == 0 else z + j
            @pl.when(block >= 0 if way == 0 else block < n_view)
            def _():
                v_hop(way, j, block, h).wait_recv()
                if j < n_view - 1:
                    @pl.when(v_can(way))
                    def _():
                        v_hop(way, j + 1, block, h).start()
                if h == 1:
                    prepare_block(block)

    def prepare_images(off):
        c = ring.chip(off)
        for h in (0, 1):
            ring.cross_wait(off, h)
        hi, lo = split(img[pl.ds(2 * c, 2)].reshape(2 * rows, feats))
        ihi[c] = hi
        ilo[c] = lo

    prepare_block(z)

    def score(off):
        c = ring.chip(off)
        s = dot_nt(vhi[...], ihi[c]) + dot_nt(vhi[...], ilo[c]) + dot_nt(vlo[...], ihi[c])
        s = beta * (s - hn[:, 0:1])
        top = jnp.max(s, axis=0, keepdims=True)
        e = jnp.exp(s - top)
        expo[c] = e
        stats[c, 0:1, :] = top
        stats[c, 1:2, :] = jnp.sum(e, axis=0, keepdims=True)

    v_events = [(j, h) for j in range(1, n_view) for h in (0, 1)]
    i_events = [(s, second) for s in range(1, chips // 2 + 1) for second in (0, 1)
                if s < chips // 2 or not second]
    order = []
    order += [("v", v) for v in v_events[:4]] + [("i", e) for e in i_events[:1]]
    order += [("v", v) for v in v_events[4:]] + [("i", e) for e in i_events[1:]]
    views_left = len(v_events)
    ready = [0]

    def flush():
        while ready:
            off = ready.pop(0)
            if off:
                prepare_images(off)
            score(off)

    for kind, what in order:
        if kind == "v":
            v_arrive(*what)
            if views_left == len(v_events):
                prepare_images(0)
            views_left -= 1
            if views_left == 0:
                flush()
        else:
            s, second = what
            ring.arrive(0, s, second)
            ring.arrive(1, s, 1 - second)
            if s == chips // 2:
                ready += [s]
            elif second:
                ready += [-s, s]
            if views_left == 0:
                flush()

    sent = []
    for d in range(1, n_img):
        copy = pltpu.make_async_remote_copy(
            stats, seen.at[d - 1], st_send.at[d - 1], st_recv.at[d - 1],
            device_id=(lax.rem(i + d, n_img), z), device_id_type=MESH)
        copy.start()
        sent.append(copy)
    for copy in sent:
        copy.wait_recv()
    mass = jnp.zeros((n_view * part, 1), F32)
    for c in range(chips):
        mine = stats[c, 0:1, :]
        peak = mine
        for d in range(n_img - 1):
            peak = jnp.maximum(peak, seen[d, c, 0:1, :])
        factor = jnp.exp(mine - peak)
        total = stats[c, 1:2, :] * factor
        for d in range(n_img - 1):
            total = total + seen[d, c, 1:2, :] * jnp.exp(seen[d, c, 0:1, :] - peak)
        post = expo[c] * (factor / total)
        mass = mass + jnp.sum(post, axis=1, keepdims=True)
        hi, lo = split(post)
        phi[c] = hi
        plo[c] = lo

    eye = (lax.broadcasted_iota(jnp.int32, (part, 128), 0)
           == lax.broadcasted_iota(jnp.int32, (part, 128), 1))
    for b in range(n_view):
        col = mass[b * part:(b + 1) * part]
        row = jnp.sum(jnp.where(eye, col, 0.0), axis=0, keepdims=True)
        mrow[b] = jnp.broadcast_to(row, (8, 128))
    m_sent = []
    for d in range(1, n_view):
        to = lax.rem(z + d, n_view)
        copy = pltpu.make_async_remote_copy(
            mrow.at[to], mrx.at[d - 1], m_send.at[d - 1], m_recv.at[d - 1],
            device_id=(i, to), device_id_type=MESH)
        copy.start()
        m_sent.append(copy)

    r_sent = []

    def numerators(h):
        total = jnp.zeros((n_view * part, width), F32)
        cols = pl.ds(h * width, width)
        for c in range(chips):
            total = total + (dot_nn(phi[c], ihi[c, :, cols]) + dot_nn(phi[c], ilo[c, :, cols])
                             + dot_nn(plo[c], ihi[c, :, cols]))
        num[h] = total.reshape(n_view, part, width)
        for d in range(1, n_view):
            to = lax.rem(z + d, n_view)
            copy = pltpu.make_async_remote_copy(
                num.at[h, to], rx.at[h, d - 1], r_send.at[h, d - 1], r_recv.at[h, d - 1],
                device_id=(i, to), device_id_type=MESH)
            copy.start()
            r_sent.append(copy)

    out_ring = Ring(chips, pos, core, z, res, PIECES, oring_send, oring_recv, osib_send, osib_recv)

    def summed(h):
        total = num[h, z]
        for d in range(n_view - 1):
            r_sent[h * (n_view - 1) + d].wait_recv()
            total = total + rx[h, d]
        return total

    def mass_total():
        for copy in m_sent:
            copy.wait_recv()
        row = mrow[z, 0:1, :]
        for d in range(n_view - 1):
            row = row + mrx[d, 0:1, :]
        return jnp.sum(jnp.where(eye, row, 0.0), axis=1, keepdims=True)

    def gather(h):
        for off in range(1, chips):
            out_ring.direct(off, h, False).wait_recv()
            out_ring.go(out_ring.cross(-off, core, h))

    for h in range(PIECES):
        numerators(h)
    mass_all = mass_total()
    for h in range(PIECES):
        current = vws[z, :, pl.ds(h * width, width)]
        res[i, :, pl.ds(h * width, width)] = current + (summed(h) - mass_all * current) / (mass_all + 1.0)
        for off in range(1, chips):
            out_ring.go(out_ring.direct(off, h, True))
        out_ring.go(out_ring.cross(0, core, h))
        if h > 0:
            gather(h - 1)
    gather(PIECES - 1)

    stores = []
    for off in range(chips):
        for h in range(PIECES):
            out_ring.cross_wait(-off, h)
        c = out_ring.chip(-off)
        copy = pltpu.make_async_copy(res.at[pl.ds(2 * c, 2)], out_ref.at[pl.ds(2 * c, 2)], out_sem.at[off])
        copy.start()
        stores.append(copy)

    ring.finish()
    out_ring.finish()
    for way in (0, 1):
        for j in range(1, n_view):
            block = z - (j - 1) if way == 0 else z + (j - 1)

            @pl.when(jnp.logical_and(v_can(way), block >= 0 if way == 0 else block < n_view))
            def _():
                for h in (0, 1):
                    v_hop(way, j, block, h).wait_send()
    for copy in sent + m_sent + r_sent:
        copy.wait_send()
    for copy in stores:
        copy.wait()


def on_device(n_img, n_view, images, views):
    inner, batch, feats = images.shape
    rows = inner * batch
    chips = n_img // 2
    part = views.shape[0] // n_img
    mine = n_view * part
    beta = 1.6 / math.sqrt(feats)
    width = feats // PIECES
    dma = pltpu.SemaphoreType.DMA
    vmem = pltpu.VMEM
    ring_sems = [dma((2, chips // 2, 2)), dma((2, chips // 2, 2)), dma((chips, 2)), dma((chips, 2))]
    out = pl.pallas_call(
        functools.partial(kernel, n_img, n_view, beta),
        out_shape=jax.ShapeDtypeStruct((n_img, part, feats), F32),
        in_specs=[pl.BlockSpec(memory_space=pl.ANY)] * 2,
        out_specs=pl.BlockSpec(memory_space=pl.ANY),
        scratch_shapes=[
            vmem((n_img, rows, feats), F32),
            vmem((chips, 2 * rows, feats), BF16),
            vmem((chips, 2 * rows, feats), BF16),
            vmem((n_view, part, feats), F32),
            vmem((mine, feats), BF16),
            vmem((mine, feats), BF16),
            vmem((mine, 128), F32),
            vmem((chips, mine, 2 * rows), F32),
            vmem((chips, mine, 2 * rows), BF16),
            vmem((chips, mine, 2 * rows), BF16),
            vmem((chips, 2, 2 * rows), F32),
            vmem((n_img - 1, chips, 2, 2 * rows), F32),
            vmem((PIECES, n_view, part, width), F32),
            vmem((PIECES, n_view - 1, part, width), F32),
            vmem((n_view, 8, 128), F32),
            vmem((n_view - 1, 8, 128), F32),
            vmem((n_img, part, feats), F32),
            dma((2,)), dma((chips,)),
        ] + ring_sems + [
            dma((chips - 1, PIECES)), dma((chips - 1, PIECES)), dma((chips, PIECES)), dma((chips, PIECES))] + [
            dma((2, n_view - 1, 2)), dma((2, n_view - 1, 2)),
            dma((n_img - 1,)), dma((n_img - 1,)),
            dma((PIECES, n_view - 1)), dma((PIECES, n_view - 1)),
            dma((n_view - 1,)), dma((n_view - 1,)),
        ],
        compiler_params=pltpu.CompilerParams(
            collective_id=0, has_side_effects=True, vmem_limit_bytes=51 * 1024 * 1024),
        cost_estimate=pl.CostEstimate(
            flops=12 * mine * n_img * rows * feats, bytes_accessed=16 * rows * feats, transcendentals=0),
    )(images.reshape(rows, feats), views)
    return out.reshape(n_img * part, feats)


def solution(mesh):
    placed = (P(None, ("img", "view"), None), P("view", None))
    return jax.shard_map(
        functools.partial(on_device, mesh.shape["img"], mesh.shape["view"]),
        mesh=mesh, in_specs=placed, out_specs=P("view", None), check_vma=False)
```
